256 devices in a mesh: dp: 64 (over y_lo, x, z), mp: 2 (over y_hi), teach: 2 (over core).
Axes of the slice: x: 4, y: 4 (y_hi: 2, y_lo: 2; y = y_hi * 2 + y_lo), z: 8, core: 2. Of those that a mesh axis runs over, the one named last changes fastest.
Arguments:
- image_feats: bfloat16 [8192, 768], P('dp'), may hold values from -6 to 6
- student_text: bfloat16 [8192, 768], P(('dp', 'mp')), may hold values from -40 to 40
- student_head: bfloat16 [768, 768], P(None, 'mp'), may hold values from -2 to 2
- teacher_image: bfloat16 [8192, 1024], P(('dp', 'teach')), may hold values from -6 to 6
- teacher_text: bfloat16 [8192, 1024], P(('dp', 'mp', 'teach')), may hold values from -40 to 40
- group_index: int32 [64], P('dp'), may hold values from 0 to 3
Outputs:
- row_loss: float32 [8192], P('dp')
- image_grad: bfloat16 [8192, 768], P('dp', 'mp')
- text_grad: bfloat16 [8192, 768], P(('dp', 'mp'))
- weight_grad: float32 [768, 768], P(None, 'mp')
The draws below stay inside these ranges and needn't reach their ends.
All inputs are finite; a program needn't handle non-finite values.
Results may differ from the reference program's by a relative error of at most 0.015.
Values may be sent and summed in bfloat16 or wider, within the bound.
No kernel may reach another device: no remote copies, remote signals or barrier semaphores. Data moves between devices by JAX's collectives and lax.ppermute only.
A program may use at most 64 MiB of HBM per device.

```python
import math
import jax
import jax.numpy as jnp
from jax import lax

D_S = 768
D_T = 1024
ROWS = 128
GROUP_ROWS = 32
GROUPS = 4
PAIRS = 8192
N_DP = 64


def draw_image_feats(key, part):
    key = jax.random.fold_in(key, 1)
    drawn = jnp.clip(jax.random.normal(key, (PAIRS, D_S), jnp.float32), -6.0, 6.0)
    return drawn.astype(jnp.bfloat16)


def draw_student_text(key, part):
    key = jax.random.fold_in(key, 2)
    drawn = jnp.clip(jax.random.normal(key, (PAIRS, D_S), jnp.float32), -6.0, 6.0)
    return drawn.astype(jnp.bfloat16)


def draw_student_head(key, part):
    key = jax.random.fold_in(key, 3)
    noise = jnp.clip(jax.random.normal(key, (D_S, D_S), jnp.float32), -6.0, 6.0) / jnp.sqrt(jnp.float32(D_S))
    return noise.astype(jnp.bfloat16)


def draw_teacher_image(key, part):
    key = jax.random.fold_in(key, 4)
    drawn = jnp.clip(jax.random.normal(key, (PAIRS, D_T), jnp.float32), -6.0, 6.0)
    return drawn.astype(jnp.bfloat16)


def draw_teacher_text(key, part):
    key = jax.random.fold_in(key, 5)
    drawn = jnp.clip(jax.random.normal(key, (PAIRS, D_T), jnp.float32), -6.0, 6.0)
    return drawn.astype(jnp.bfloat16)


def set_ends(array, rng, smallest, largest):
    spot = [jax.random.randint(jax.random.fold_in(rng, axis), (), 0, length) for axis, length in enumerate(array.shape)]
    main_axis = array.shape.index(max(array.shape))
    neighbour = spot[:main_axis] + [(spot[main_axis] + 1) % array.shape[main_axis]] + spot[main_axis + 1:]
    return array.at[tuple(spot)].set(smallest).at[tuple(neighbour)].set(largest)


def setup_inputs(seed: int = 0) -> dict:
    seeds = jax.random.split(jax.random.key(seed), 7)
    return {
        "image_feats": draw_image_feats(jax.random.fold_in(seeds[6], 71), 0),
        "student_text": draw_student_text(jax.random.fold_in(seeds[6], 71), 0),
        "student_head": draw_student_head(jax.random.fold_in(seeds[6], 71), 0),
        "teacher_image": draw_teacher_image(jax.random.fold_in(seeds[6], 71), 0),
        "teacher_text": draw_teacher_text(jax.random.fold_in(seeds[6], 71), 0),
        "group_index": set_ends(jax.random.randint(seeds[5], (N_DP,), 0, GROUPS), jax.random.fold_in(seeds[5], 1), 0, GROUPS - 1).astype(jnp.int32),
    }


epsilon = 1e-06
loss_scale = 8.0

def reference(image_feats, student_text, student_head, teacher_image, teacher_text, group_index):
    pair_count, model_width = image_feats.shape
    student_scale = 3.0 / math.sqrt(model_width)
    teacher_scale = 3.0 / math.sqrt(teacher_image.shape[1])
    projected = jnp.dot(image_feats, student_head, preferred_element_type=jnp.float32)
    row_factor = lax.rsqrt(lax.optimization_barrier(jnp.sum(projected * projected, axis=1, keepdims=True)) / model_width + epsilon)
    queries = (projected * row_factor).astype(jnp.bfloat16)
    row_block = 512 if pair_count % 512 == 0 else pair_count
    block_count = pair_count // row_block

    def panel_step(column_sum, block_index):
        first_row = (block_index * row_block).astype(jnp.int32)
        query_block = lax.dynamic_slice_in_dim(queries, first_row, row_block, 0)
        teacher_block = lax.dynamic_slice_in_dim(teacher_image, first_row, row_block, 0)
        student = student_scale * jnp.dot(query_block, student_text.T, preferred_element_type=jnp.float32)
        teacher = teacher_scale * jnp.dot(teacher_block, teacher_text.T, preferred_element_type=jnp.float32)
        top_t = lax.optimization_barrier(jnp.max(teacher, axis=1, keepdims=True))
        weights = jnp.exp(teacher - top_t)
        total_t = lax.optimization_barrier(jnp.sum(weights, axis=1, keepdims=True))
        cross_term = lax.optimization_barrier(jnp.sum(weights * (teacher - student), axis=1, keepdims=True))
        top_s = lax.optimization_barrier(jnp.max(student, axis=1, keepdims=True))
        total_s = lax.optimization_barrier(jnp.sum(jnp.exp(student - top_s), axis=1, keepdims=True))
        lse_t = top_t + jnp.log(total_t)
        lse_s = top_s + jnp.log(total_s)
        losses = cross_term / total_t - lse_t + lse_s
        logit_slope = (loss_scale * (jnp.exp(student - lse_s) - jnp.exp(teacher - lse_t))).astype(jnp.bfloat16)
        query_grad = student_scale * jnp.dot(logit_slope, student_text, preferred_element_type=jnp.float32)
        column_sum = column_sum + student_scale * jnp.dot(logit_slope.T, query_block, preferred_element_type=jnp.float32)
        return (column_sum, (losses[:, 0], query_grad))
    start_sum = jnp.zeros((pair_count, model_width), jnp.float32)
    column_sum, (losses, grads) = lax.scan(panel_step, start_sum, jnp.arange(block_count, dtype=jnp.int32))
    row_loss = losses.reshape(pair_count)
    query_grad = grads.reshape(pair_count, model_width)
    first_rows = (group_index * GROUP_ROWS).astype(jnp.int32)

    def block_rows(values):
        stacked = values.reshape(N_DP, ROWS, values.shape[-1])
        picked = jax.vmap(lambda rows_of, start: lax.dynamic_slice_in_dim(rows_of, start, GROUP_ROWS, 0))(stacked, first_rows)
        return picked.reshape(N_DP * GROUP_ROWS, values.shape[-1])
    group_feats = block_rows(image_feats)
    group_proj = block_rows(projected)
    group_factor = block_rows(row_factor)
    group_grad = block_rows(query_grad)
    inner_sum = lax.optimization_barrier(jnp.sum(group_grad * group_proj, axis=1, keepdims=True))
    head_slope = (group_factor * group_grad - group_factor * group_factor * group_factor * group_proj * inner_sum / model_width).astype(jnp.bfloat16)
    weight_grad = jnp.dot(group_feats.T, head_slope, preferred_element_type=jnp.float32)
    return (row_loss, query_grad.astype(jnp.bfloat16), column_sum.astype(jnp.bfloat16), weight_grad)
```

```python
import math

import jax
import jax.numpy as jnp
from jax import lax
from jax.sharding import Mesh, PartitionSpec as P

epsilon = 1e-06
loss_scale = 8.0

COLS = ("x", "yl", "yh")
bf16, f32 = jnp.bfloat16, jnp.float32


def to_all(value, axes, count):
    sent = jnp.broadcast_to(value[None], (count, *value.shape))
    return lax.all_to_all(sent, axes, 0, 0, tiled=True)


def pick(value, index, axis):
    return lax.dynamic_index_in_dim(value, index, axis, keepdims=False)


def swap(value, axis):
    return lax.ppermute(value, axis, [(0, 1), (1, 0)])


def sent_round(value):
    return [lax.ppermute(value, "z", [(i, (i + k) % 8) for i in range(8)]) for k in range(1, 8)]


def dot(left, right, left_dim, right_dim):
    return lax.dot_general(
        left, right, (((left_dim,), (right_dim,)), ((), ())), preferred_element_type=f32
    )


def shards(image_feats, student_text, student_head, teacher_image, teacher_text, group_index):
    core, high, here = lax.axis_index("c"), lax.axis_index("yh"), lax.axis_index("z")
    width, wide = student_head.shape[0], teacher_image.shape[1]
    half = width // 2
    student_scale, teacher_scale = 3.0 / math.sqrt(width), 3.0 / math.sqrt(wide)
    group = group_index[0]

    def block_first(value):
        return lax.dynamic_slice_in_dim(jnp.concatenate([value, value], 0), group, 4, 0)

    text_own = pick(student_text.reshape(2, 32, width), core, 0)
    cols_own = jnp.concatenate([text_own, teacher_text], 1)

    teach = pick(teacher_image.reshape(2, 2, 2, 8, wide), high, 1)
    keep, come = pick(teach, core, 1), swap(pick(teach, 1 - core, 1), "c")
    teach_own = jnp.where(core == 0, jnp.stack([keep, come]), jnp.stack([come, keep])).reshape(4, 8, wide)
    feats_own = pick(pick(image_feats.reshape(4, 2, 2, 8, width), high, 1), core, 1)
    own = block_first(jnp.concatenate([feats_own, teach_own], 2)).reshape(32, width + wide)
    sent = jnp.broadcast_to(cols_own[None], (16, 32, width + wide))
    cols = lax.all_to_all(sent, COLS, 0, 0, tiled=True)
    head_come = swap(pick(student_head.reshape(2, half, half), core, 0), "yh")
    cols, head_come, *round_z = lax.optimization_barrier((cols, head_come, *sent_round(own)))
    cols = cols.reshape(512, width + wide)
    rows_own = jnp.zeros((8, 32, width + wide), bf16)
    for k, block in enumerate([own] + round_z):
        rows_own = lax.dynamic_update_slice_in_dim(rows_own, block[None], (here - k) % 8, 0)
    block_z = rows_own[:, :8, :width].reshape(64, width)
    rows_own = rows_own.reshape(256, width + wide)
    block_all = to_all(block_z, COLS, 16).reshape(1024, width)

    rows_come, head_pair = swap(rows_own, "c"), swap(head_come, "c")
    head_other = jnp.where(
        core == 0, jnp.concatenate([head_come, head_pair], 0), jnp.concatenate([head_pair, head_come], 0)
    )
    head = jnp.where(
        high == 0,
        jnp.concatenate([student_head, head_other], 1),
        jnp.concatenate([head_other, student_head], 1),
    )
    text, teach = cols[:, :width], cols[:, width:]
    rows = jnp.concatenate([rows_own, rows_come], 0)

    projected = dot(rows[:, :width], head, 1, 0)
    factor = lax.rsqrt(jnp.sum(projected * projected, axis=1, keepdims=True) / width + epsilon)
    queries = (projected * factor).astype(bf16)
    student = student_scale * dot(text, queries, 1, 1)
    teacher = teacher_scale * dot(teach, rows[:, width:], 1, 1)
    top_t = jnp.max(teacher, axis=0)
    weights = jnp.exp(teacher - top_t)
    total_t = jnp.sum(weights, axis=0)
    cross = jnp.sum(weights * (teacher - student), axis=0)
    top_s = jnp.max(student, axis=0)
    total_s = jnp.sum(jnp.exp(student - top_s), axis=0)
    zero = jnp.zeros_like(top_t)

    def merged(stats):
        tops_t, totals_t, crosses, tops_s, totals_s = (stats[:, i] for i in range(5))
        high_t, high_s = jnp.max(tops_t, axis=0), jnp.max(tops_s, axis=0)
        shift_t = jnp.exp(tops_t - high_t)
        sum_t = jnp.sum(totals_t * shift_t, axis=0)
        sum_s = jnp.sum(totals_s * jnp.exp(tops_s - high_s), axis=0)
        sum_cross = jnp.sum(crosses * shift_t, axis=0)
        return jnp.stack([high_t, sum_t, sum_cross, high_s, sum_s, zero, zero, zero])

    stats = jnp.stack([top_t, total_t, cross, top_s, total_s, zero, zero, zero])
    block_all, *round_z = lax.optimization_barrier((block_all, *sent_round(stats)))
    stats = merged(jnp.stack([stats] + round_z))
    come = swap(stats, "c")
    come = jnp.concatenate([come[:, 256:], come[:, :256]], 1)
    high_t, sum_t, sum_cross, high_s, sum_s = merged(jnp.stack([stats, come]))[:5]
    lse_t, lse_s = high_t + jnp.log(sum_t), high_s + jnp.log(sum_s)
    losses = sum_cross / sum_t - lse_t + lse_s

    slope = (loss_scale * (jnp.exp(student - lse_s) - jnp.exp(teacher - lse_t))).astype(bf16)
    grad = student_scale * dot(slope, text, 0, 0)
    text_part = (student_scale * dot(slope, queries, 1, 0)).astype(bf16)

    grad = grad[:256] + swap(grad[256:].astype(bf16), "c").astype(f32)
    grad = grad.astype(bf16).reshape(8, 32, width)
    blocks = grad[:, :8].reshape(64, width)
    turned = lax.dynamic_slice_in_dim(jnp.concatenate([grad, grad], 0), here, 8, 0)[:, 8:]
    round_z = [
        lax.ppermute(jnp.concatenate([turned[k], blocks], 0), "z", [(i, (i + k) % 8) for i in range(8)])
        for k in range(1, 8)
    ]
    text_part = lax.all_to_all(text_part.reshape(16, 32, width), COLS, 0, 0, tiled=True)
    text_part, *round_z = lax.optimization_barrier((text_part, *round_z))
    grad = jnp.concatenate([turned[0], blocks], 0).astype(f32) + sum(r.astype(f32) for r in round_z)
    block_grad = grad[24:]
    grad = jnp.concatenate([pick(block_grad.reshape(8, 8, width), here, 0), grad[:24]], 0)

    block_proj = dot(block_z, head, 1, 0)
    block_factor = lax.rsqrt(jnp.sum(block_proj * block_proj, axis=1, keepdims=True) / width + epsilon)
    inner = jnp.sum(block_grad * block_proj, axis=1, keepdims=True)
    head_slope = (
        block_factor * block_grad
        - block_factor * block_factor * block_factor * block_proj * inner / width
    ).astype(bf16)
    head_slope = head_slope.reshape(64, 2, half).transpose(1, 0, 2)

    sent = jnp.broadcast_to(head_slope[None], (8, 2, 64, half)).reshape(16, 64, half)
    slopes = lax.all_to_all(sent, COLS, 0, 0, tiled=True)

    text_sum = jnp.sum(text_part.astype(f32), axis=0).astype(bf16)
    text_grad = lax.all_gather(text_sum, "c", axis=0, tiled=True)

    back = lambda value: lax.dynamic_slice_in_dim(jnp.concatenate([value, value], 0), 4 - group, 4, 0)
    halves = back(grad.astype(bf16).reshape(4, 8, width)).reshape(32, 2, half)
    mine, come = pick(halves, high, 1), swap(pick(halves, 1 - high, 1), "yh")
    pair = jnp.where(high == 0, jnp.stack([mine, come]), jnp.stack([come, mine]))
    pair = lax.all_gather(pair, "c", axis=0)
    image_grad = pair.reshape(2, 2, 4, 8, half).transpose(2, 1, 0, 3, 4).reshape(128, half)

    losses = pick(losses.reshape(2, 8, 4, 8), here, 1)
    losses = jnp.where(core == 0, losses, losses[::-1])
    losses = back(losses.transpose(1, 0, 2))
    come = swap(losses, "yh")
    row_loss = jnp.where(high == 0, jnp.stack([losses, come], 1), jnp.stack([come, losses], 1)).reshape(128)
    slopes, row_loss, image_grad, text_grad = lax.optimization_barrier(
        (slopes, row_loss, image_grad, text_grad)
    )
    part = dot(block_all, slopes.reshape(1024, half), 0, 0)
    weight_grad = part + swap(part.astype(bf16), "c").astype(f32)
    return row_loss, image_grad, text_grad, weight_grad


def solution(mesh):
    mesh = Mesh(mesh.devices.reshape(2, 4, 8, 2, 2), ("yl", "x", "z", "yh", "c"))
    dp = ("yl", "x", "z")
    in_specs = (
        P(dp, None),
        P((*dp, "yh"), None),
        P(None, "yh"),
        P((*dp, "c"), None),
        P((*dp, "yh", "c"), None),
        P(dp),
    )
    out_specs = (P(dp), P(dp, "yh"), P((*dp, "yh"), None), P(None, "yh"))
    return jax.shard_map(shards, mesh=mesh, in_specs=in_specs, out_specs=out_specs, check_vma=False)
```

```python
import math

import jax
import jax.numpy as jnp
from jax import lax
from jax.experimental import pallas as pl
from jax.experimental.pallas import tpu as pltpu
from jax.sharding import Mesh, PartitionSpec as P

epsilon = 1e-06
loss_scale = 8.0

COLS = ("x", "yl", "yh")
bf16, f32 = jnp.bfloat16, jnp.float32


def to_all(value, axes, count):
    sent = jnp.broadcast_to(value[None], (count, *value.shape))
    return lax.all_to_all(sent, axes, 0, 0, tiled=True)


def pick(value, index, axis):
    return lax.dynamic_index_in_dim(value, index, axis, keepdims=False)


def swap(value, axis):
    return lax.ppermute(value, axis, [(0, 1), (1, 0)])


def turn(value, k):
    pairs = [(2 * i, 2 * ((i + k) % 8)) for i in range(8)]
    pairs += [(2 * i + 1, 2 * ((i - k) % 8) + 1) for i in range(8)]
    return lax.ppermute(value, ("z", "c"), pairs)


def in_order(here, core, whole, halves):
    order = sorted(whole)
    rows, width = halves[0].shape

    def kernel(here_ref, core_ref, *refs):
        out_ref, here, core = refs[-1], here_ref[0], core_ref[0]
        sign = 1 - 2 * core
        for place, ref in zip(order, refs):
            z = (here + sign * place + 8) % 8
            for i in range(2):
                first = pl.multiple_of((core + i) % 2 * rows, rows)
                out_ref[i, z] = ref[pl.ds(first, rows), :]
        for i in range(2):
            out_ref[i, (here + 4) % 8] = refs[len(order) + i][...]

    blocks = [whole[place] for place in order] + list(halves)
    return pl.pallas_call(
        kernel,
        out_shape=jax.ShapeDtypeStruct((2, 8, rows, width), halves[0].dtype),
        in_specs=[pl.BlockSpec(memory_space=pltpu.SMEM)] * 2
        + [pl.BlockSpec(memory_space=pltpu.VMEM)] * len(blocks),
        out_specs=pl.BlockSpec(memory_space=pltpu.VMEM),
        compiler_params=pltpu.CompilerParams(vmem_limit_bytes=16 * 2**20),
    )(here.reshape(1).astype(jnp.int32), core.reshape(1).astype(jnp.int32), *blocks)


def copies(core, text, teach, count):
    rows, width, wide = teach.shape[0], text.shape[1], teach.shape[1]

    def kernel(core_ref, text_ref, teach_ref, out_ref):
        first = pl.multiple_of(core_ref[0] * rows, rows)
        text, teach = text_ref[pl.ds(first, rows), :], teach_ref[...]
        for i in range(count):
            out_ref[i, :, :width] = text
            out_ref[i, :, width:] = teach

    return pl.pallas_call(
        kernel,
        out_shape=jax.ShapeDtypeStruct((count, rows, width + wide), text.dtype),
        in_specs=[
            pl.BlockSpec(memory_space=pltpu.SMEM),
            pl.BlockSpec(memory_space=pltpu.VMEM),
            pl.BlockSpec(memory_space=pltpu.VMEM),
        ],
        out_specs=pl.BlockSpec(memory_space=pltpu.VMEM),
        compiler_params=pltpu.CompilerParams(vmem_limit_bytes=16 * 2**20),
    )(core.reshape(1).astype(jnp.int32), text, teach)


def dot(left, right, left_dim, right_dim):
    return lax.dot_general(
        left, right, (((left_dim,), (right_dim,)), ((), ())), preferred_element_type=f32
    )


def shards(image_feats, student_text, student_head, teacher_image, teacher_text, group_index):
    core, high, here = lax.axis_index("c"), lax.axis_index("yh"), lax.axis_index("z")
    width, wide = student_head.shape[0], teacher_image.shape[1]
    half = width // 2
    student_scale, teacher_scale = 3.0 / math.sqrt(width), 3.0 / math.sqrt(wide)
    group = group_index[0]

    def block_first(value):
        return lax.dynamic_slice_in_dim(jnp.concatenate([value, value], 0), group, 4, 0)


    teach = pick(teacher_image.reshape(2, 2, 16, wide), high, 1)
    come = swap(teach, "c")
    teach = jnp.where(core == 0, jnp.stack([teach, come]), jnp.stack([come, teach])).reshape(4, 2, 8, wide)
    feats = pick(image_feats.reshape(4, 2, 2, 8, width), high, 1)
    own = block_first(jnp.concatenate([feats, teach], 3))
    own = own.transpose(1, 0, 2, 3).reshape(64, width + wide)
    sent = copies(core, student_text, teacher_text, 16)
    head_come = pick(student_head.reshape(2, half, half), core, 0)
    head_come = lax.ppermute(head_come, ("yl", "yh"), [(i, 3 - i) for i in range(4)])
    sent, head_come = lax.optimization_barrier((sent, head_come))
    cols = lax.all_to_all(sent, COLS, 0, 0, tiled=True)
    near = {k: turn(own, k) for k in (3, 1, 2)}
    far = turn(pick(near[3].reshape(2, 32, width + wide), core, 0), 1)
    head_pair = swap(head_come, "c")
    opposite = {k: swap(near[k], "c") for k in (3, 1, 2)}
    beyond = swap(far, "c")
    cols, head_pair, near, opposite, far, beyond = lax.optimization_barrier(
        (cols, head_pair, near, opposite, far, beyond)
    )
    cols = cols.reshape(512, width + wide)
    whole = {0: own} | {-k: near[k] for k in near} | {k: opposite[k] for k in opposite}
    rows = in_order(here, core, whole, (far, beyond)).reshape(512, width + wide)
    head_other = jnp.where(
        core == 0, jnp.concatenate([head_come, head_pair], 0), jnp.concatenate([head_pair, head_come], 0)
    )
    head = jnp.where(
        high == 0,
        jnp.concatenate([student_head, head_other], 1),
        jnp.concatenate([head_other, student_head], 1),
    )
    text, teach = cols[:, :width], cols[:, width:]

    projected = dot(rows[:, :width], head, 1, 0)
    factor = lax.rsqrt(jnp.sum(projected * projected, axis=1, keepdims=True) / width + epsilon)
    queries = (projected * factor).astype(bf16)
    student = student_scale * dot(text, queries, 1, 1)
    teacher = teacher_scale * dot(teach, rows[:, width:], 1, 1)
    top_t = jnp.max(teacher, axis=0)
    weights = jnp.exp(teacher - top_t)
    total_t = jnp.sum(weights, axis=0)
    cross = jnp.sum(weights * (teacher - student), axis=0)
    top_s = jnp.max(student, axis=0)
    total_s = jnp.sum(jnp.exp(student - top_s), axis=0)
    zero = jnp.zeros_like(top_t)

    def merged(stats):
        tops_t, totals_t, crosses, tops_s, totals_s = (stats[:, i] for i in range(5))
        high_t, high_s = jnp.max(tops_t, axis=0), jnp.max(tops_s, axis=0)
        shift_t = jnp.exp(tops_t - high_t)
        sum_t = jnp.sum(totals_t * shift_t, axis=0)
        sum_s = jnp.sum(totals_s * jnp.exp(tops_s - high_s), axis=0)
        sum_cross = jnp.sum(crosses * shift_t, axis=0)
        return jnp.stack([high_t, sum_t, sum_cross, high_s, sum_s, zero, zero, zero])

    stats = jnp.stack([top_t, total_t, cross, top_s, total_s, zero, zero, zero])
    stats = merged(to_all(stats, "z", 8))
    come = swap(stats, "c")
    come = jnp.concatenate([come[:, 256:], come[:, :256]], 1)
    high_t, sum_t, sum_cross, high_s, sum_s = merged(jnp.stack([stats, come]))[:5]
    lse_t, lse_s = high_t + jnp.log(sum_t), high_s + jnp.log(sum_s)
    losses = sum_cross / sum_t - lse_t + lse_s

    slope = (loss_scale * (jnp.exp(student - lse_s) - jnp.exp(teacher - lse_t))).astype(bf16)
    grad = student_scale * dot(slope, text, 0, 0)
    text_part = (student_scale * dot(slope, queries, 1, 0)).astype(bf16)

    def blocks(value):
        return value.reshape(2, 8, 32, value.shape[1])[:, :, :8].reshape(128, value.shape[1])

    block_grad, block_proj, block_factor = blocks(grad), blocks(projected), blocks(factor)
    inner = jnp.sum(block_grad * block_proj, axis=1, keepdims=True)
    head_slope = (
        block_factor * block_grad
        - block_factor * block_factor * block_factor * block_proj * inner / width
    ).astype(bf16)
    share = dot(blocks(rows[:, :width]), head_slope, 0, 0).reshape(2, half, width)
    share = pick(share, core, 0) + swap(pick(share, 1 - core, 0).astype(bf16), "c").astype(f32)
    share = share.astype(bf16).reshape(16, 24, width)

    grad = grad[:256] + swap(grad[256:].astype(bf16), "c").astype(f32)
    grad = grad.astype(bf16).reshape(8, 32, width)
    turned = lax.dynamic_slice_in_dim(jnp.concatenate([grad, grad], 0), here, 8, 0)
    round_z = [
        lax.ppermute(turned[k], "z", [(i, (i + k) % 8) for i in range(8)]) for k in range(1, 8)
    ]
    sent = jnp.concatenate([text_part.reshape(16, 32, width), share], 1)
    sent = lax.all_to_all(sent, COLS, 0, 0, tiled=True)
    sent, losses, *round_z = lax.optimization_barrier((sent, losses, *round_z))
    grad = turned[0].astype(f32) + sum(r.astype(f32) for r in round_z)
    share = jnp.sum(sent[:, 32:].astype(f32), axis=0).astype(bf16)
    share = to_all(share, "z", 8)

    def back(value):
        return lax.dynamic_slice_in_dim(jnp.concatenate([value, value], 0), 4 - group, 4, 0)

    text_sum = jnp.sum(sent[:, :32].astype(f32), axis=0).astype(bf16)
    text_grad = lax.all_gather(text_sum, "c", axis=0, tiled=True)
    halves = back(grad.astype(bf16).reshape(4, 8, width)).reshape(32, 2, half)
    grad_come = swap(pick(halves, 1 - high, 1), "yh")
    losses = pick(losses.reshape(2, 8, 4, 8), here, 1)
    losses = jnp.where(core == 0, losses, losses[::-1])
    losses = back(losses.transpose(1, 0, 2))
    losses_come = swap(losses, "yh")
    share, text_grad, grad_come, losses_come = lax.optimization_barrier(
        (share, text_grad, grad_come, losses_come)
    )

    share = jnp.sum(share.astype(f32), axis=0).astype(bf16)
    share = share.reshape(24, 2, half).transpose(1, 0, 2)
    share = jnp.broadcast_to(share[None], (8, 2, 24, half)).reshape(16, 24, half)
    share = lax.all_to_all(share, COLS, 0, 0, tiled=True).reshape(half, half)

    mine = pick(halves, high, 1)
    pair = jnp.where(high == 0, jnp.stack([mine, grad_come]), jnp.stack([grad_come, mine]))
    pair = lax.all_gather(pair, "c", axis=0)
    image_grad = pair.reshape(2, 2, 4, 8, half).transpose(2, 1, 0, 3, 4).reshape(128, half)
    row_loss = jnp.where(
        high == 0, jnp.stack([losses, losses_come], 1), jnp.stack([losses_come, losses], 1)
    ).reshape(128)
    share, row_loss, image_grad = lax.optimization_barrier((share, row_loss, image_grad))
    weight_grad = lax.all_gather(share, "c", axis=0, tiled=True).astype(f32)
    return row_loss, image_grad, text_grad, weight_grad


def solution(mesh):
    mesh = Mesh(mesh.devices.reshape(2, 4, 8, 2, 2), ("yl", "x", "z", "yh", "c"))
    dp = ("yl", "x", "z")
    in_specs = (
        P(dp, None),
        P((*dp, "yh"), None),
        P(None, "yh"),
        P((*dp, "c"), None),
        P((*dp, "yh", "c"), None),
        P(dp),
    )
    out_specs = (P(dp), P(dp, "yh"), P((*dp, "yh"), None), P(None, "yh"))
    return jax.shard_map(shards, mesh=mesh, in_specs=in_specs, out_specs=out_specs, check_vma=False)
```

```python
import math

import jax
import jax.numpy as jnp
from jax import lax
from jax.experimental import pallas as pl
from jax.experimental.pallas import tpu as pltpu
from jax.sharding import Mesh, PartitionSpec as P

epsilon = 1e-06
loss_scale = 8.0

COLS = ("x", "yl", "yh")
bf16, f32 = jnp.bfloat16, jnp.float32


def to_all(value, axes, count):
    sent = jnp.broadcast_to(value[None], (count, *value.shape))
    return lax.all_to_all(sent, axes, 0, 0, tiled=True)


def pick(value, index, axis):
    return lax.dynamic_index_in_dim(value, index, axis, keepdims=False)


def swap(value, axis):
    return lax.ppermute(value, axis, [(0, 1), (1, 0)])


def turn(value, k):
    pairs = [(2 * i, 2 * ((i + k) % 8)) for i in range(8)]
    pairs += [(2 * i + 1, 2 * ((i - k) % 8) + 1) for i in range(8)]
    return lax.ppermute(value, ("z", "c"), pairs)


def in_order(here, core, whole, halves):
    order = sorted(whole)
    rows, width = halves[0].shape

    def kernel(here_ref, core_ref, *refs):
        out_ref, here, core = refs[-1], here_ref[0], core_ref[0]
        sign = 1 - 2 * core
        for place, ref in zip(order, refs):
            z = (here + sign * place + 8) % 8
            for i in range(2):
                first = pl.multiple_of((core + i) % 2 * rows, rows)
                out_ref[i, z] = ref[pl.ds(first, rows), :]
        for i in range(2):
            out_ref[i, (here + 4) % 8] = refs[len(order) + i][...]

    blocks = [whole[place] for place in order] + list(halves)
    return pl.pallas_call(
        kernel,
        out_shape=jax.ShapeDtypeStruct((2, 8, rows, width), halves[0].dtype),
        in_specs=[pl.BlockSpec(memory_space=pltpu.SMEM)] * 2
        + [pl.BlockSpec(memory_space=pltpu.VMEM)] * len(blocks),
        out_specs=pl.BlockSpec(memory_space=pltpu.VMEM),
        compiler_params=pltpu.CompilerParams(vmem_limit_bytes=16 * 2**20),
    )(here.reshape(1).astype(jnp.int32), core.reshape(1).astype(jnp.int32), *blocks)


def copies(core, text, teach, count):
    rows, width, wide = teach.shape[0], text.shape[1], teach.shape[1]

    def kernel(core_ref, text_ref, teach_ref, out_ref):
        first = pl.multiple_of(core_ref[0] * rows, rows)
        text, teach = text_ref[pl.ds(first, rows), :], teach_ref[...]
        for i in range(count):
            out_ref[i, :, :width] = text
            out_ref[i, :, width:] = teach

    return pl.pallas_call(
        kernel,
        out_shape=jax.ShapeDtypeStruct((count, rows, width + wide), text.dtype),
        in_specs=[
            pl.BlockSpec(memory_space=pltpu.SMEM),
            pl.BlockSpec(memory_space=pltpu.VMEM),
            pl.BlockSpec(memory_space=pltpu.VMEM),
        ],
        out_specs=pl.BlockSpec(memory_space=pltpu.VMEM),
        compiler_params=pltpu.CompilerParams(vmem_limit_bytes=16 * 2**20),
    )(core.reshape(1).astype(jnp.int32), text, teach)


def dot(left, right, left_dim, right_dim):
    return lax.dot_general(
        left, right, (((left_dim,), (right_dim,)), ((), ())), preferred_element_type=f32
    )


def shards(image_feats, student_text, student_head, teacher_image, teacher_text, group_index):
    core, high, here = lax.axis_index("c"), lax.axis_index("yh"), lax.axis_index("z")
    width, wide = student_head.shape[0], teacher_image.shape[1]
    half = width // 2
    student_scale, teacher_scale = 3.0 / math.sqrt(width), 3.0 / math.sqrt(wide)
    group = group_index[0]

    def block_first(value):
        return lax.dynamic_slice_in_dim(jnp.concatenate([value, value], 0), group, 4, 0)


    teach = pick(teacher_image.reshape(2, 2, 16, wide), high, 1)
    come = swap(teach, "c")
    teach = jnp.where(core == 0, jnp.stack([teach, come]), jnp.stack([come, teach])).reshape(4, 2, 8, wide)
    feats = pick(image_feats.reshape(4, 2, 2, 8, width), high, 1)
    own = block_first(jnp.concatenate([feats, teach], 3))
    own = own.transpose(1, 0, 2, 3).reshape(64, width + wide)
    sent = copies(core, student_text, teacher_text, 16)
    head_come = pick(student_head.reshape(2, half, half), core, 0)
    head_come = lax.ppermute(head_come, ("yl", "yh"), [(i, 3 - i) for i in range(4)])
    sent, head_come = lax.optimization_barrier((sent, head_come))
    cols = lax.all_to_all(sent, COLS, 0, 0, tiled=True)
    near = {k: turn(own, k) for k in (3, 1, 2)}
    far = turn(pick(near[3].reshape(2, 32, width + wide), core, 0), 1)
    head_pair = swap(head_come, "c")
    opposite = {k: swap(near[k], "c") for k in (3, 1, 2)}
    beyond = swap(far, "c")
    cols, head_pair, near, opposite, far, beyond = lax.optimization_barrier(
        (cols, head_pair, near, opposite, far, beyond)
    )
    cols = cols.reshape(512, width + wide)
    whole = {0: own} | {-k: near[k] for k in near} | {k: opposite[k] for k in opposite}
    rows = in_order(here, core, whole, (far, beyond)).reshape(512, width + wide)
    head_other = jnp.where(
        core == 0, jnp.concatenate([head_come, head_pair], 0), jnp.concatenate([head_pair, head_come], 0)
    )
    head = jnp.where(
        high == 0,
        jnp.concatenate([student_head, head_other], 1),
        jnp.concatenate([head_other, student_head], 1),
    )
    text, teach = cols[:, :width], cols[:, width:]

    projected = dot(rows[:, :width], head, 1, 0)
    factor = lax.rsqrt(jnp.sum(projected * projected, axis=1, keepdims=True) / width + epsilon)
    queries = (projected * factor).astype(bf16)
    student = student_scale * dot(text, queries, 1, 1)
    teacher = teacher_scale * dot(teach, rows[:, width:], 1, 1)
    top_t = jnp.max(teacher, axis=0)
    weights = jnp.exp(teacher - top_t)
    total_t = jnp.sum(weights, axis=0)
    cross = jnp.sum(weights * (teacher - student), axis=0)
    top_s = jnp.max(student, axis=0)
    total_s = jnp.sum(jnp.exp(student - top_s), axis=0)
    zero = jnp.zeros_like(top_t)

    def merged(stats):
        tops_t, totals_t, crosses, tops_s, totals_s = (stats[:, i] for i in range(5))
        high_t, high_s = jnp.max(tops_t, axis=0), jnp.max(tops_s, axis=0)
        shift_t = jnp.exp(tops_t - high_t)
        sum_t = jnp.sum(totals_t * shift_t, axis=0)
        sum_s = jnp.sum(totals_s * jnp.exp(tops_s - high_s), axis=0)
        sum_cross = jnp.sum(crosses * shift_t, axis=0)
        return jnp.stack([high_t, sum_t, sum_cross, high_s, sum_s, zero, zero, zero])

    stats = jnp.stack([top_t, total_t, cross, top_s, total_s, zero, zero, zero])
    stats = merged(to_all(stats, "z", 8))
    come = swap(stats, "c")
    come = jnp.concatenate([come[:, 256:], come[:, :256]], 1)
    high_t, sum_t, sum_cross, high_s, sum_s = merged(jnp.stack([stats, come]))[:5]
    lse_t, lse_s = high_t + jnp.log(sum_t), high_s + jnp.log(sum_s)
    losses = sum_cross / sum_t - lse_t + lse_s

    slope = (loss_scale * (jnp.exp(student - lse_s) - jnp.exp(teacher - lse_t))).astype(bf16)
    grad = student_scale * dot(slope, text, 0, 0)
    text_part = (student_scale * dot(slope, queries, 1, 0)).astype(bf16)

    def blocks(value):
        return value.reshape(2, 8, 32, value.shape[1])[:, :, :8].reshape(128, value.shape[1])

    block_grad, block_proj, block_factor = blocks(grad), blocks(projected), blocks(factor)
    inner = jnp.sum(block_grad * block_proj, axis=1, keepdims=True)
    head_slope = (
        block_factor * block_grad
        - block_factor * block_factor * block_factor * block_proj * inner / width
    ).astype(bf16)
    share = dot(blocks(rows[:, :width]), head_slope, 0, 0).reshape(2, half, width)
    share = pick(share, core, 0) + swap(pick(share, 1 - core, 0).astype(bf16), "c").astype(f32)
    share = share.astype(bf16).reshape(8, 2, 24, width)
    share = [
        jnp.concatenate([share[:, 0, :, columns], share[:, 1, :, columns]], 2)
        for columns in (slice(0, half), slice(half, width))
    ]
    share = jnp.stack(share, 1).reshape(16, 24, width)

    grad = grad[:256] + swap(grad[256:].astype(bf16), "c").astype(f32)
    grad = grad.astype(bf16).reshape(8, 32, width)
    turned = lax.dynamic_slice_in_dim(jnp.concatenate([grad, grad], 0), here, 8, 0)
    round_z = [
        lax.ppermute(turned[k], "z", [(i, (i + k) % 8) for i in range(8)]) for k in range(1, 8)
    ]
    sent = jnp.concatenate([text_part.reshape(16, 32, width), share], 1)
    sent = lax.all_to_all(sent, COLS, 0, 0, tiled=True)
    sent, losses, *round_z = lax.optimization_barrier((sent, losses, *round_z))
    grad = turned[0].astype(f32) + sum(r.astype(f32) for r in round_z)
    share = jnp.sum(sent[:, 32:].astype(f32), axis=0).astype(bf16)
    share = to_all(share, "z", 8)

    def back(value):
        return lax.dynamic_slice_in_dim(jnp.concatenate([value, value], 0), 4 - group, 4, 0)

    text_sum = jnp.sum(sent[:, :32].astype(f32), axis=0).astype(bf16)
    text_come = swap(text_sum, "c")
    halves = back(grad.astype(bf16).reshape(4, 8, width)).reshape(32, 2, half)
    grad_come = swap(pick(halves, 1 - high, 1), "yh")
    losses = pick(losses.reshape(2, 8, 4, 8), here, 1)
    losses = jnp.where(core == 0, losses, losses[::-1])
    losses = back(losses.transpose(1, 0, 2))
    losses_come = swap(losses, "yh")
    share, text_come, grad_come, losses_come = lax.optimization_barrier(
        (share, text_come, grad_come, losses_come)
    )

    share = jnp.sum(share.astype(f32), axis=0).astype(bf16)
    share = jnp.concatenate([share[:, :half], share[:, half:]], 0)
    share = to_all(share, ("x", "yl"), 8).reshape(half, half)

    mine = pick(halves, high, 1)
    pair = jnp.where(high == 0, jnp.stack([mine, grad_come]), jnp.stack([grad_come, mine]))
    pair_come = swap(pair, "c")
    pair = jnp.where(core == 0, jnp.stack([pair, pair_come]), jnp.stack([pair_come, pair]))
    image_grad = pair.reshape(2, 2, 4, 8, half).transpose(2, 1, 0, 3, 4).reshape(128, half)
    text_grad = jnp.where(
        core == 0, jnp.concatenate([text_sum, text_come], 0), jnp.concatenate([text_come, text_sum], 0)
    )
    row_loss = jnp.where(
        high == 0, jnp.stack([losses, losses_come], 1), jnp.stack([losses_come, losses], 1)
    ).reshape(128)
    share, row_loss, image_grad, text_grad = lax.optimization_barrier(
        (share, row_loss, image_grad, text_grad)
    )
    weight_grad = lax.all_gather(share, "c", axis=0, tiled=True).astype(f32)
    return row_loss, image_grad, text_grad, weight_grad


def solution(mesh):
    mesh = Mesh(mesh.devices.reshape(2, 4, 8, 2, 2), ("yl", "x", "z", "yh", "c"))
    dp = ("yl", "x", "z")
    in_specs = (
        P(dp, None),
        P((*dp, "yh"), None),
        P(None, "yh"),
        P((*dp, "c"), None),
        P((*dp, "yh", "c"), None),
        P(dp),
    )
    out_specs = (P(dp), P(dp, "yh"), P((*dp, "yh"), None), P(None, "yh"))
    return jax.shard_map(shards, mesh=mesh, in_specs=in_specs, out_specs=out_specs, check_vma=False)
```

```python
import math

import jax
import jax.numpy as jnp
from jax import lax
from jax.experimental import pallas as pl
from jax.experimental.pallas import tpu as pltpu
from jax.sharding import Mesh, PartitionSpec as P

epsilon = 1e-06
loss_scale = 8.0

COLS = ("x", "yl", "yh")
bf16, f32 = jnp.bfloat16, jnp.float32


def to_all(value, axes, count):
    sent = jnp.broadcast_to(value[None], (count, *value.shape))
    return lax.all_to_all(sent, axes, 0, 0, tiled=True)


def pick(value, index, axis):
    return lax.dynamic_index_in_dim(value, index, axis, keepdims=False)


def swap(value, axis):
    return lax.ppermute(value, axis, [(0, 1), (1, 0)])


def turn(value, k):
    pairs = [(2 * i, 2 * ((i + k) % 8)) for i in range(8)]
    pairs += [(2 * i + 1, 2 * ((i - k) % 8) + 1) for i in range(8)]
    return lax.ppermute(value, ("z", "c"), pairs)


def in_order(here, core, whole, halves):
    order = sorted(whole)
    rows, width = halves[0].shape

    def kernel(here_ref, core_ref, *refs):
        out_ref, here, core = refs[-1], here_ref[0], core_ref[0]
        sign = 1 - 2 * core
        for place, ref in zip(order, refs):
            z = (here + sign * place + 8) % 8
            for i in range(2):
                first = pl.multiple_of((core + i) % 2 * rows, rows)
                out_ref[i, z] = ref[pl.ds(first, rows), :]
        for i in range(2):
            out_ref[i, (here + 4) % 8] = refs[len(order) + i][...]

    blocks = [whole[place] for place in order] + list(halves)
    return pl.pallas_call(
        kernel,
        out_shape=jax.ShapeDtypeStruct((2, 8, rows, width), halves[0].dtype),
        in_specs=[pl.BlockSpec(memory_space=pltpu.SMEM)] * 2
        + [pl.BlockSpec(memory_space=pltpu.VMEM)] * len(blocks),
        out_specs=pl.BlockSpec(memory_space=pltpu.VMEM),
        compiler_params=pltpu.CompilerParams(vmem_limit_bytes=16 * 2**20),
    )(here.reshape(1).astype(jnp.int32), core.reshape(1).astype(jnp.int32), *blocks)


def copies(core, text, teach, count):
    rows, width, wide = teach.shape[0], text.shape[1], teach.shape[1]

    def kernel(core_ref, text_ref, teach_ref, out_ref):
        first = pl.multiple_of(core_ref[0] * rows, rows)
        text, teach = text_ref[pl.ds(first, rows), :], teach_ref[...]
        for i in range(count):
            out_ref[i, :, :width] = text
            out_ref[i, :, width:] = teach

    return pl.pallas_call(
        kernel,
        out_shape=jax.ShapeDtypeStruct((count, rows, width + wide), text.dtype),
        in_specs=[
            pl.BlockSpec(memory_space=pltpu.SMEM),
            pl.BlockSpec(memory_space=pltpu.VMEM),
            pl.BlockSpec(memory_space=pltpu.VMEM),
        ],
        out_specs=pl.BlockSpec(memory_space=pltpu.VMEM),
        compiler_params=pltpu.CompilerParams(vmem_limit_bytes=16 * 2**20),
    )(core.reshape(1).astype(jnp.int32), text, teach)


def dot(left, right, left_dim, right_dim):
    return lax.dot_general(
        left, right, (((left_dim,), (right_dim,)), ((), ())), preferred_element_type=f32
    )


def shards(image_feats, student_text, student_head, teacher_image, teacher_text, group_index):
    core, high, here = lax.axis_index("c"), lax.axis_index("yh"), lax.axis_index("z")
    width, wide = student_head.shape[0], teacher_image.shape[1]
    half = width // 2
    student_scale, teacher_scale = 3.0 / math.sqrt(width), 3.0 / math.sqrt(wide)
    group = group_index[0]

    def block_first(value):
        return lax.dynamic_slice_in_dim(jnp.concatenate([value, value], 0), group, 4, 0)


    teach = pick(teacher_image.reshape(2, 2, 16, wide), high, 1)
    come = swap(teach, "c")
    teach = jnp.where(core == 0, jnp.stack([teach, come]), jnp.stack([come, teach])).reshape(4, 2, 8, wide)
    feats = pick(image_feats.reshape(4, 2, 2, 8, width), high, 1)
    own = block_first(jnp.concatenate([feats, teach], 3))
    own = own.transpose(1, 0, 2, 3).reshape(64, width + wide)
    sent = copies(core, student_text, teacher_text, 16)
    head_come = pick(student_head.reshape(2, half, half), core, 0)
    head_come = lax.ppermute(head_come, ("yl", "yh"), [(i, 3 - i) for i in range(4)])
    sent, head_come = lax.optimization_barrier((sent, head_come))
    cols = lax.all_to_all(sent, COLS, 0, 0, tiled=True)
    near = {k: turn(own, k) for k in (3, 1, 2)}
    far = turn(pick(near[3].reshape(2, 32, width + wide), core, 0), 1)
    head_pair = swap(head_come, "c")
    opposite = {k: swap(near[k], "c") for k in (3, 1, 2)}
    beyond = swap(far, "c")
    cols, head_pair, near, opposite, far, beyond = lax.optimization_barrier(
        (cols, head_pair, near, opposite, far, beyond)
    )
    cols = cols.reshape(512, width + wide)
    whole = {0: own} | {-k: near[k] for k in near} | {k: opposite[k] for k in opposite}
    rows = in_order(here, core, whole, (far, beyond)).reshape(512, width + wide)
    head_other = jnp.where(
        core == 0, jnp.concatenate([head_come, head_pair], 0), jnp.concatenate([head_pair, head_come], 0)
    )
    head = jnp.where(
        high == 0,
        jnp.concatenate([student_head, head_other], 1),
        jnp.concatenate([head_other, student_head], 1),
    )
    text, teach = cols[:, :width], cols[:, width:]

    projected = dot(rows[:, :width], head, 1, 0)
    factor = lax.rsqrt(jnp.sum(projected * projected, axis=1, keepdims=True) / width + epsilon)
    queries = (projected * factor).astype(bf16)
    student = student_scale * dot(text, queries, 1, 1)
    teacher = teacher_scale * dot(teach, rows[:, width:], 1, 1)
    top_t = jnp.max(teacher, axis=0)
    weights = jnp.exp(teacher - top_t)
    total_t = jnp.sum(weights, axis=0)
    cross = jnp.sum(weights * (teacher - student), axis=0)
    top_s = jnp.max(student, axis=0)
    total_s = jnp.sum(jnp.exp(student - top_s), axis=0)
    zero = jnp.zeros_like(top_t)

    def merged(stats):
        tops_t, totals_t, crosses, tops_s, totals_s = (stats[:, i] for i in range(5))
        high_t, high_s = jnp.max(tops_t, axis=0), jnp.max(tops_s, axis=0)
        shift_t = jnp.exp(tops_t - high_t)
        sum_t = jnp.sum(totals_t * shift_t, axis=0)
        sum_s = jnp.sum(totals_s * jnp.exp(tops_s - high_s), axis=0)
        sum_cross = jnp.sum(crosses * shift_t, axis=0)
        return jnp.stack([high_t, sum_t, sum_cross, high_s, sum_s, zero, zero, zero])

    stats = jnp.stack([top_t, total_t, cross, top_s, total_s, zero, zero, zero])
    stats = merged(to_all(stats, "z", 8))
    come = swap(stats, "c")
    come = jnp.concatenate([come[:, 256:], come[:, :256]], 1)
    high_t, sum_t, sum_cross, high_s, sum_s = merged(jnp.stack([stats, come]))[:5]
    lse_t, lse_s = high_t + jnp.log(sum_t), high_s + jnp.log(sum_s)
    losses = sum_cross / sum_t - lse_t + lse_s

    slope = (loss_scale * (jnp.exp(student - lse_s) - jnp.exp(teacher - lse_t))).astype(bf16)
    grad = student_scale * dot(slope, text, 0, 0)
    text_part = (student_scale * dot(slope, queries, 1, 0)).astype(bf16)

    def blocks(value):
        return value.reshape(2, 8, 32, value.shape[1])[:, :, :8].reshape(128, value.shape[1])

    block_grad, block_proj, block_factor = blocks(grad), blocks(projected), blocks(factor)
    inner = jnp.sum(block_grad * block_proj, axis=1, keepdims=True)
    head_slope = (
        block_factor * block_grad
        - block_factor * block_factor * block_factor * block_proj * inner / width
    ).astype(bf16)
    share = dot(blocks(rows[:, :width]), head_slope, 0, 0).reshape(2, half, width)
    share = pick(share, core, 0) + swap(pick(share, 1 - core, 0).astype(bf16), "c").astype(f32)
    share = share.astype(bf16).reshape(8, 2, 24, width)
    share = [
        jnp.concatenate([share[:, 0, :, columns], share[:, 1, :, columns]], 2)
        for columns in (slice(0, half), slice(half, width))
    ]
    share = jnp.stack(share, 1).reshape(16, 24, width)

    grad = grad[:256] + swap(grad[256:].astype(bf16), "c").astype(f32)
    grad = grad.astype(bf16).reshape(8, 32, width)
    turned = lax.dynamic_slice_in_dim(jnp.concatenate([grad, grad], 0), here, 8, 0)
    round_z = [
        lax.ppermute(turned[k], "z", [(i, (i + k) % 8) for i in range(8)]) for k in range(1, 8)
    ]
    sent = jnp.concatenate([text_part.reshape(16, 32, width), share], 1)
    sent = lax.all_to_all(sent, COLS, 0, 0, tiled=True)
    sent, losses = lax.optimization_barrier((sent, losses))
    grad = turned[0].astype(f32) + sum(r.astype(f32) for r in round_z)
    share = jnp.sum(sent[:, 32:].astype(f32), axis=0).astype(bf16)
    share = to_all(share, "z", 8)

    def back(value):
        return lax.dynamic_slice_in_dim(jnp.concatenate([value, value], 0), 4 - group, 4, 0)

    text_sum = jnp.sum(sent[:, :32].astype(f32), axis=0).astype(bf16)
    text_come = swap(text_sum, "c")
    halves = back(grad.astype(bf16).reshape(4, 8, width)).reshape(32, 2, half)
    grad_come = swap(pick(halves, 1 - high, 1), "yh")
    losses = pick(losses.reshape(2, 8, 4, 8), here, 1)
    losses = jnp.where(core == 0, losses, losses[::-1])
    losses = back(losses.transpose(1, 0, 2))
    losses_come = swap(losses, "yh")
    share, text_come, grad_come, losses_come = lax.optimization_barrier(
        (share, text_come, grad_come, losses_come)
    )

    share = jnp.sum(share.astype(f32), axis=0).astype(bf16)
    share = jnp.concatenate([share[:, :half], share[:, half:]], 0)
    share = to_all(share, ("x", "yl"), 8).reshape(half, half)

    mine = pick(halves, high, 1)
    pair = jnp.where(high == 0, jnp.stack([mine, grad_come]), jnp.stack([grad_come, mine]))
    pair_come = swap(pair, "c")
    pair = jnp.where(core == 0, jnp.stack([pair, pair_come]), jnp.stack([pair_come, pair]))
    image_grad = pair.reshape(2, 2, 4, 8, half).transpose(2, 1, 0, 3, 4).reshape(128, half)
    text_grad = jnp.where(
        core == 0, jnp.concatenate([text_sum, text_come], 0), jnp.concatenate([text_come, text_sum], 0)
    )
    row_loss = jnp.where(
        high == 0, jnp.stack([losses, losses_come], 1), jnp.stack([losses_come, losses], 1)
    ).reshape(128)
    share, row_loss, image_grad, text_grad = lax.optimization_barrier(
        (share, row_loss, image_grad, text_grad)
    )
    come = swap(share, "c")
    weight_grad = jnp.where(
        core == 0, jnp.concatenate([share, come], 0), jnp.concatenate([come, share], 0)
    ).astype(f32)
    return row_loss, image_grad, text_grad, weight_grad


def solution(mesh):
    mesh = Mesh(mesh.devices.reshape(2, 4, 8, 2, 2), ("yl", "x", "z", "yh", "c"))
    dp = ("yl", "x", "z")
    in_specs = (
        P(dp, None),
        P((*dp, "yh"), None),
        P(None, "yh"),
        P((*dp, "c"), None),
        P((*dp, "yh", "c"), None),
        P(dp),
    )
    out_specs = (P(dp), P(dp, "yh"), P((*dp, "yh"), None), P(None, "yh"))
    return jax.shard_map(shards, mesh=mesh, in_specs=in_specs, out_specs=out_specs, check_vma=False)
```

```python
import math

import jax
import jax.numpy as jnp
from jax import lax
from jax.experimental import pallas as pl
from jax.experimental.pallas import tpu as pltpu
from jax.sharding import Mesh, PartitionSpec as P

epsilon = 1e-06
loss_scale = 8.0

COLS = ("x", "yl", "yh")
bf16, f32 = jnp.bfloat16, jnp.float32


def to_all(value, axes, count):
    sent = jnp.broadcast_to(value[None], (count, *value.shape))
    return lax.all_to_all(sent, axes, 0, 0, tiled=True)


def pick(value, index, axis):
    return lax.dynamic_index_in_dim(value, index, axis, keepdims=False)


def swap(value, axis):
    return lax.ppermute(value, axis, [(0, 1), (1, 0)])


def turn(value, k):
    pairs = [(2 * i, 2 * ((i + k) % 8)) for i in range(8)]
    pairs += [(2 * i + 1, 2 * ((i - k) % 8) + 1) for i in range(8)]
    return lax.ppermute(value, ("z", "c"), pairs)


def in_order(here, core, whole, halves):
    order = sorted(whole)
    rows, width = halves[0].shape

    def kernel(here_ref, core_ref, *refs):
        out_ref, here, core = refs[-1], here_ref[0], core_ref[0]
        sign = 1 - 2 * core
        for place, ref in zip(order, refs):
            z = (here + sign * place + 8) % 8
            for i in range(2):
                first = pl.multiple_of((core + i) % 2 * rows, rows)
                out_ref[i, z] = ref[pl.ds(first, rows), :]
        for i in range(2):
            out_ref[i, (here + 4) % 8] = refs[len(order) + i][...]

    blocks = [whole[place] for place in order] + list(halves)
    return pl.pallas_call(
        kernel,
        out_shape=jax.ShapeDtypeStruct((2, 8, rows, width), halves[0].dtype),
        in_specs=[pl.BlockSpec(memory_space=pltpu.SMEM)] * 2
        + [pl.BlockSpec(memory_space=pltpu.VMEM)] * len(blocks),
        out_specs=pl.BlockSpec(memory_space=pltpu.VMEM),
        compiler_params=pltpu.CompilerParams(vmem_limit_bytes=16 * 2**20),
    )(here.reshape(1).astype(jnp.int32), core.reshape(1).astype(jnp.int32), *blocks)


def copies(core, text, teach, count):
    rows, width, wide = teach.shape[0], text.shape[1], teach.shape[1]

    def kernel(core_ref, text_ref, teach_ref, out_ref):
        first = pl.multiple_of(core_ref[0] * rows, rows)
        text, teach = text_ref[pl.ds(first, rows), :], teach_ref[...]
        for i in range(count):
            out_ref[i, :, :width] = text
            out_ref[i, :, width:] = teach

    return pl.pallas_call(
        kernel,
        out_shape=jax.ShapeDtypeStruct((count, rows, width + wide), text.dtype),
        in_specs=[
            pl.BlockSpec(memory_space=pltpu.SMEM),
            pl.BlockSpec(memory_space=pltpu.VMEM),
            pl.BlockSpec(memory_space=pltpu.VMEM),
        ],
        out_specs=pl.BlockSpec(memory_space=pltpu.VMEM),
        compiler_params=pltpu.CompilerParams(vmem_limit_bytes=16 * 2**20),
    )(core.reshape(1).astype(jnp.int32), text, teach)


def dot(left, right, left_dim, right_dim):
    return lax.dot_general(
        left, right, (((left_dim,), (right_dim,)), ((), ())), preferred_element_type=f32
    )


def shards(image_feats, student_text, student_head, teacher_image, teacher_text, group_index):
    core, high, here = lax.axis_index("c"), lax.axis_index("yh"), lax.axis_index("z")
    width, wide = student_head.shape[0], teacher_image.shape[1]
    half = width // 2
    student_scale, teacher_scale = 3.0 / math.sqrt(width), 3.0 / math.sqrt(wide)
    group = group_index[0]

    def block_first(value):
        return lax.dynamic_slice_in_dim(jnp.concatenate([value, value], 0), group, 4, 0)


    teach = pick(teacher_image.reshape(2, 2, 16, wide), high, 1)
    sent = copies(core, student_text, teacher_text, 16)
    head_come = pick(student_head.reshape(2, half, half), core, 0)
    head_come = lax.ppermute(head_come, ("yl", "yh"), [(i, 3 - i) for i in range(4)])
    sent, head_come, come = lax.optimization_barrier((sent, head_come, swap(teach, "c")))
    teach = jnp.where(core == 0, jnp.stack([teach, come]), jnp.stack([come, teach])).reshape(4, 2, 8, wide)
    feats = pick(image_feats.reshape(4, 2, 2, 8, width), high, 1)
    own = block_first(jnp.concatenate([feats, teach], 3))
    own = own.transpose(1, 0, 2, 3).reshape(64, width + wide)
    cols = lax.all_to_all(sent, COLS, 0, 0, tiled=True)
    near = {k: turn(own, k) for k in (3, 1, 2)}
    far = turn(pick(near[3].reshape(2, 32, width + wide), core, 0), 1)
    head_pair = swap(head_come, "c")
    opposite = {k: swap(near[k], "c") for k in (3, 1, 2)}
    beyond = swap(far, "c")
    cols, head_pair, near, opposite, far, beyond = lax.optimization_barrier(
        (cols, head_pair, near, opposite, far, beyond)
    )
    cols = cols.reshape(512, width + wide)
    whole = {0: own} | {-k: near[k] for k in near} | {k: opposite[k] for k in opposite}
    rows = in_order(here, core, whole, (far, beyond)).reshape(512, width + wide)
    head_other = jnp.where(
        core == 0, jnp.concatenate([head_come, head_pair], 0), jnp.concatenate([head_pair, head_come], 0)
    )
    head = jnp.where(
        high == 0,
        jnp.concatenate([student_head, head_other], 1),
        jnp.concatenate([head_other, student_head], 1),
    )
    text, teach = cols[:, :width], cols[:, width:]

    projected = dot(rows[:, :width], head, 1, 0)
    factor = lax.rsqrt(jnp.sum(projected * projected, axis=1, keepdims=True) / width + epsilon)
    queries = (projected * factor).astype(bf16)
    student = student_scale * dot(text, queries, 1, 1)
    teacher = teacher_scale * dot(teach, rows[:, width:], 1, 1)
    top_t = jnp.max(teacher, axis=0)
    weights = jnp.exp(teacher - top_t)
    total_t = jnp.sum(weights, axis=0)
    cross = jnp.sum(weights * (teacher - student), axis=0)
    top_s = jnp.max(student, axis=0)
    total_s = jnp.sum(jnp.exp(student - top_s), axis=0)
    zero = jnp.zeros_like(top_t)

    def merged(stats):
        tops_t, totals_t, crosses, tops_s, totals_s = (stats[:, i] for i in range(5))
        high_t, high_s = jnp.max(tops_t, axis=0), jnp.max(tops_s, axis=0)
        shift_t = jnp.exp(tops_t - high_t)
        sum_t = jnp.sum(totals_t * shift_t, axis=0)
        sum_s = jnp.sum(totals_s * jnp.exp(tops_s - high_s), axis=0)
        sum_cross = jnp.sum(crosses * shift_t, axis=0)
        return jnp.stack([high_t, sum_t, sum_cross, high_s, sum_s, zero, zero, zero])

    stats = jnp.stack([top_t, total_t, cross, top_s, total_s, zero, zero, zero])
    stats = merged(to_all(stats, "z", 8))
    come = swap(stats, "c")
    come = jnp.concatenate([come[:, 256:], come[:, :256]], 1)
    high_t, sum_t, sum_cross, high_s, sum_s = merged(jnp.stack([stats, come]))[:5]
    lse_t, lse_s = high_t + jnp.log(sum_t), high_s + jnp.log(sum_s)
    losses = sum_cross / sum_t - lse_t + lse_s

    slope = (loss_scale * (jnp.exp(student - lse_s) - jnp.exp(teacher - lse_t))).astype(bf16)
    grad = student_scale * dot(slope, text, 0, 0)
    text_part = (student_scale * dot(slope, queries, 1, 0)).astype(bf16)

    def blocks(value):
        return value.reshape(2, 8, 32, value.shape[1])[:, :, :8].reshape(128, value.shape[1])

    block_grad, block_proj, block_factor = blocks(grad), blocks(projected), blocks(factor)
    inner = jnp.sum(block_grad * block_proj, axis=1, keepdims=True)
    head_slope = (
        block_factor * block_grad
        - block_factor * block_factor * block_factor * block_proj * inner / width
    ).astype(bf16)
    share = dot(blocks(rows[:, :width]), head_slope, 0, 0).reshape(2, half, width)
    share = pick(share, core, 0) + swap(pick(share, 1 - core, 0).astype(bf16), "c").astype(f32)
    share = share.astype(bf16).reshape(8, 2, 24, width)
    share = [
        jnp.concatenate([share[:, 0, :, columns], share[:, 1, :, columns]], 2)
        for columns in (slice(0, half), slice(half, width))
    ]
    share = jnp.stack(share, 1).reshape(16, 24, width)

    grad = grad[:256] + swap(grad[256:].astype(bf16), "c").astype(f32)
    grad = grad.astype(bf16).reshape(8, 32, width)
    turned = lax.dynamic_slice_in_dim(jnp.concatenate([grad, grad], 0), here, 8, 0)
    round_z = [
        lax.ppermute(turned[k], "z", [(i, (i + k) % 8) for i in range(8)]) for k in range(1, 8)
    ]
    sent = jnp.concatenate([text_part.reshape(16, 32, width), share], 1)
    sent = lax.all_to_all(sent, COLS, 0, 0, tiled=True)
    sent, losses = lax.optimization_barrier((sent, losses))
    grad = turned[0].astype(f32) + sum(r.astype(f32) for r in round_z)
    share = jnp.sum(sent[:, 32:].astype(f32), axis=0).astype(bf16)
    share = to_all(share, "z", 8)

    def back(value):
        return lax.dynamic_slice_in_dim(jnp.concatenate([value, value], 0), 4 - group, 4, 0)

    text_sum = jnp.sum(sent[:, :32].astype(f32), axis=0).astype(bf16)
    text_come = swap(text_sum, "c")
    halves = back(grad.astype(bf16).reshape(4, 8, width)).reshape(32, 2, half)
    grad_come = swap(pick(halves, 1 - high, 1), "yh")
    losses = pick(losses.reshape(2, 8, 4, 8), here, 1)
    losses = jnp.where(core == 0, losses, losses[::-1])
    losses = back(losses.transpose(1, 0, 2))
    losses_come = swap(losses, "yh")
    share, text_come, grad_come, losses_come = lax.optimization_barrier(
        (share, text_come, grad_come, losses_come)
    )

    share = jnp.sum(share.astype(f32), axis=0).astype(bf16)
    share = jnp.concatenate([share[:, :half], share[:, half:]], 0)
    share = to_all(share, ("x", "yl"), 8).reshape(half, half)

    mine = pick(halves, high, 1)
    pair = jnp.where(high == 0, jnp.stack([mine, grad_come]), jnp.stack([grad_come, mine]))
    pair_come = swap(pair, "c")
    pair = jnp.where(core == 0, jnp.stack([pair, pair_come]), jnp.stack([pair_come, pair]))
    image_grad = pair.reshape(2, 2, 4, 8, half).transpose(2, 1, 0, 3, 4).reshape(128, half)
    text_grad = jnp.where(
        core == 0, jnp.concatenate([text_sum, text_come], 0), jnp.concatenate([text_come, text_sum], 0)
    )
    row_loss = jnp.where(
        high == 0, jnp.stack([losses, losses_come], 1), jnp.stack([losses_come, losses], 1)
    ).reshape(128)
    share, row_loss, image_grad, text_grad = lax.optimization_barrier(
        (share, row_loss, image_grad, text_grad)
    )
    come = swap(share, "c")
    weight_grad = jnp.where(
        core == 0, jnp.concatenate([share, come], 0), jnp.concatenate([come, share], 0)
    ).astype(f32)
    return row_loss, image_grad, text_grad, weight_grad


def solution(mesh):
    mesh = Mesh(mesh.devices.reshape(2, 4, 8, 2, 2), ("yl", "x", "z", "yh", "c"))
    dp = ("yl", "x", "z")
    in_specs = (
        P(dp, None),
        P((*dp, "yh"), None),
        P(None, "yh"),
        P((*dp, "c"), None),
        P((*dp, "yh", "c"), None),
        P(dp),
    )
    out_specs = (P(dp), P(dp, "yh"), P((*dp, "yh"), None), P(None, "yh"))
    return jax.shard_map(shards, mesh=mesh, in_specs=in_specs, out_specs=out_specs, check_vma=False)
```
